32 devices in a mesh: dp: 2 (over core), seq: 4 (over z), head: 4 (over y, x).
Axes of the slice: x: 2, y: 2, z: 4, core: 2. Of those that a mesh axis runs over, the one named last changes fastest.
Arguments:
- queries: bfloat16 [2, 2560, 2048], P('dp', ('seq', 'head')), may hold values from -45 to 45
- key_rows: bfloat16 [2, 2560, 2048], P('dp', ('seq', 'head')), may hold values from -6 to 6
- values: bfloat16 [2, 2560, 2048], P('dp', ('seq', 'head')), may hold values from -6 to 6
- rand_blocks: int32 [40, 16, 4], P('seq', 'head'), may hold values from 0 to 39, as said below
- out_weight: bfloat16 [2048, 2048], P('head'), may hold values from -0.125 to 0.125
- cotangent: bfloat16 [2, 2560, 2048], P('dp', ('seq', 'head')), may hold values from -6 to 6
Outputs:
- layer_out: bfloat16 [2, 2560, 2048], P('dp', ('seq', 'head'))
- grad_queries: bfloat16 [2, 2560, 2048], P('dp', ('seq', 'head'))
- grad_keys: bfloat16 [2, 2560, 2048], P('dp', ('seq', 'head'))
- grad_values: bfloat16 [2, 2560, 2048], P('dp', ('seq', 'head'))
- weight_grad: float32 [2048, 2048], P('head')
The draws below stay inside these ranges and needn't reach their ends.
Inputs may be any that keep to these rules, and one draw needn't show every extreme that they name: `rand_blocks`: key block b lies in range b // 10 of seq. Over the 10 query blocks of one index of seq and the 4 heads of one index of head, at most 60 of the listed random blocks lie in any one range of seq; in every draw, for every index of head, some range of seq receives exactly 60 of them from every index of seq.
All inputs are finite; a program needn't handle non-finite values.
Results may differ from the reference program's by a relative error of at most 0.034.
Values may be sent and summed in bfloat16 or wider, within the bound.
A program may use at most 192 MiB of HBM per device.

```python
import math
import jax
import jax.numpy as jnp
from jax import lax

NH = 16
HEAD_SIZE = 128
BLOCK_TOKENS = 64
NRAND = 4
D = 2048
HEADS_DEV = 4
QBLK = 10
NBLK = 40
SEQLEN = 2560
DOCS = 2
SLOTS_PER_QUERY = 8
CAP = 60


def draw_queries(key, part):
    normal_field = jax.random.normal(jax.random.fold_in(key, 11), (DOCS, SEQLEN, D), jnp.float32)
    return jnp.clip(normal_field, -6.0, 6.0).astype(jnp.bfloat16)


def draw_key_rows(key, part):
    normal_field = jax.random.normal(jax.random.fold_in(key, 12), (DOCS, SEQLEN, D), jnp.float32)
    return jnp.clip(normal_field, -6.0, 6.0).astype(jnp.bfloat16)


def draw_rand_blocks(key, part):
    range_count = NBLK // QBLK
    group_count = NH // HEADS_DEV
    request_total = HEADS_DEV * QBLK * NRAND
    key_hot = jax.random.fold_in(key, 21)
    key_rest = jax.random.fold_in(key, 22)
    hot_owner = jax.random.randint(key_hot, (group_count,), 0, range_count)
    group_keys = jax.random.split(key_rest, range_count * group_count)

    def draw_group(sub_key, hot_range):
        key_pick = jax.random.fold_in(sub_key, 1)
        key_order = jax.random.fold_in(sub_key, 2)
        key_offset = jax.random.fold_in(sub_key, 3)
        picked = jax.random.permutation(key_pick, (range_count - 1) * CAP)[:request_total - CAP]
        others = (hot_range + 1 + picked // CAP) % range_count
        owners = jnp.concatenate([jnp.full((CAP,), 0, jnp.int32) + hot_range, others.astype(jnp.int32)])
        owners = jax.random.permutation(key_order, owners)
        offsets = jax.random.randint(key_offset, (request_total,), 0, QBLK)
        return (owners * QBLK + offsets).astype(jnp.int32)
    hot_all = jnp.tile(hot_owner, range_count)
    blocks = jax.vmap(draw_group)(group_keys, hot_all)
    blocks = blocks.reshape(range_count, group_count, QBLK, HEADS_DEV, NRAND)
    return jnp.transpose(blocks, (0, 2, 1, 3, 4)).reshape(NBLK, NH, NRAND).astype(jnp.int32)


def shard_levels(stream_key, shape, cuts, smallest, high):
    def one(axis_at, shards_of):
        steps = jax.random.uniform(jax.random.fold_in(jax.random.fold_in(stream_key, 6), axis_at), (shards_of,), jnp.float32, smallest / len(cuts), high / len(cuts))
        return jnp.repeat(jnp.exp(steps), shape[axis_at] // shards_of).reshape((-1,) + (1,) * (len(shape) - axis_at - 1))

    loudness = one(*cuts[0])
    for cut in cuts[1:]:
        loudness = loudness * one(*cut)
    return loudness


def normal_values(stream_key, extent, spread, reach, pieces=(), kind=jnp.bfloat16):
    array = jax.random.normal(stream_key, extent, jnp.float32) * spread
    if len(pieces) > 0:
        array = shard_levels(stream_key, extent, pieces, -0.22, 0.18) * array
    return jnp.clip(array, min=-reach, max=reach).astype(kind)


def setup_inputs(seed: int = 0) -> dict:
    key_of = jax.random.split(jax.random.key(seed), 7)
    queries = draw_queries(jax.random.fold_in(key_of[6], 71), 0)
    key_rows = draw_key_rows(jax.random.fold_in(key_of[6], 71), 0)
    values = normal_values(key_of[2], (DOCS, SEQLEN, D), 1.0, 6.0, ((0, 2), (1, 16)))
    rand_blocks = draw_rand_blocks(jax.random.fold_in(key_of[6], 71), 0)
    out_weight = normal_values(key_of[4], (D, D), D ** -0.5, 0.125, ((0, 4),))
    cotangent = normal_values(key_of[5], (DOCS, SEQLEN, D), 1.0, 6.0, ((0, 2), (1, 16)))
    return {"queries": queries, "key_rows": key_rows, "values": values, "rand_blocks": rand_blocks, "out_weight": out_weight, "cotangent": cotangent}


def rounded_length(values_in):
    return lax.optimization_barrier(values_in.astype(jnp.bfloat16)).astype(jnp.float32)

def head_pass(packed):
    query_head, key_head, value_head, grad_head, random_ids = packed
    number_of_blocks = NBLK
    softmax_scale = 1.0 / math.sqrt(HEAD_SIZE)
    query_block_rows = query_head.reshape(number_of_blocks, BLOCK_TOKENS, HEAD_SIZE).astype(jnp.float32)
    key_block_rows = key_head.reshape(number_of_blocks, BLOCK_TOKENS, HEAD_SIZE)
    value_block_rows = value_head.reshape(number_of_blocks, BLOCK_TOKENS, HEAD_SIZE)
    gradient_blocks = grad_head.reshape(number_of_blocks, BLOCK_TOKENS, HEAD_SIZE).astype(jnp.float32)
    block_ids = jnp.arange(number_of_blocks, dtype=jnp.int32)
    window = jnp.stack([jnp.maximum(block_ids - 1, 0), block_ids, jnp.minimum(block_ids + 1, number_of_blocks - 1), jnp.zeros_like(block_ids)], axis=1)
    block_per_slot = jnp.concatenate([window, random_ids.astype(jnp.int32)], axis=1)
    live_head = jnp.stack([block_ids > 0, block_ids >= 0, block_ids < number_of_blocks - 1, block_ids >= 0], axis=1)
    live_slots = jnp.concatenate([live_head, random_ids >= 0], axis=1)
    live_mask = jnp.repeat(live_slots, BLOCK_TOKENS, axis=1)[:, None, :]
    keys_per_slot = key_block_rows[block_per_slot].reshape(number_of_blocks, SLOTS_PER_QUERY * BLOCK_TOKENS, HEAD_SIZE).astype(jnp.float32)
    values_per_slot = value_block_rows[block_per_slot].reshape(number_of_blocks, SLOTS_PER_QUERY * BLOCK_TOKENS, HEAD_SIZE).astype(jnp.float32)
    scores = jnp.einsum('ibd,ikd->ibk', query_block_rows, keys_per_slot) * softmax_scale
    row_max = lax.optimization_barrier(jnp.max(jnp.where(live_mask, scores, -jnp.inf), axis=-1, keepdims=True))
    weights = jnp.where(live_mask, jnp.exp(scores - row_max), 0.0)
    totals = lax.optimization_barrier(jnp.sum(weights, axis=-1, keepdims=True))
    attn = (jnp.einsum('ibk,ikd->ibd', rounded_length(weights), values_per_slot) / totals).astype(jnp.bfloat16)
    logsum = row_max + jnp.log(totals)
    probability_rows = jnp.where(live_mask, jnp.exp(scores - logsum), 0.0)
    row_delta = lax.optimization_barrier(jnp.sum(gradient_blocks * attn.astype(jnp.float32), axis=-1, keepdims=True))
    dprob = jnp.einsum('ibd,ikd->ibk', gradient_blocks, values_per_slot)
    score_gradient = rounded_length(probability_rows * (dprob - row_delta))
    grad_q = (jnp.einsum('ibk,ikd->ibd', score_gradient, keys_per_slot) * softmax_scale).astype(jnp.bfloat16)
    key_products = (jnp.einsum('nzq,nze->nqe', score_gradient, query_block_rows) * softmax_scale).reshape(number_of_blocks, SLOTS_PER_QUERY, BLOCK_TOKENS, HEAD_SIZE)
    value_products = jnp.einsum('nzq,nze->nqe', rounded_length(probability_rows), gradient_blocks).reshape(number_of_blocks, SLOTS_PER_QUERY, BLOCK_TOKENS, HEAD_SIZE)
    key_products = jnp.concatenate([key_products[:, :4], rounded_length(key_products[:, 4:])], axis=1)
    value_products = jnp.concatenate([value_products[:, :4], rounded_length(value_products[:, 4:])], axis=1)
    grad_k = jnp.zeros((number_of_blocks, BLOCK_TOKENS, HEAD_SIZE), jnp.float32).at[block_per_slot].add(key_products)
    grad_v = jnp.zeros((number_of_blocks, BLOCK_TOKENS, HEAD_SIZE), jnp.float32).at[block_per_slot].add(value_products)
    return (attn.reshape(SEQLEN, HEAD_SIZE), grad_q.reshape(SEQLEN, HEAD_SIZE), grad_k.astype(jnp.bfloat16).reshape(SEQLEN, HEAD_SIZE), grad_v.astype(jnp.bfloat16).reshape(SEQLEN, HEAD_SIZE))

def split_heads(matrix):
    return jnp.transpose(matrix.reshape(SEQLEN, NH, HEAD_SIZE), (1, 0, 2))

def merge_heads(stacked):
    return jnp.transpose(stacked, (1, 0, 2)).reshape(SEQLEN, D)

def reference(queries, key_rows, values, rand_blocks, out_weight, cotangent):
    random_heads = jnp.transpose(rand_blocks, (1, 0, 2))
    weight_grad = jnp.zeros((D, D), jnp.float32)
    outputs, grads_q, grads_k, grads_v = ([], [], [], [])
    for doc_index in range(DOCS):
        grad_attn = jnp.dot(cotangent[doc_index], out_weight.T, preferred_element_type=jnp.float32).astype(jnp.bfloat16)
        attn_h, gq_h, gk_h, gv_h = lax.map(head_pass, (split_heads(queries[doc_index]), split_heads(key_rows[doc_index]), split_heads(values[doc_index]), split_heads(grad_attn), random_heads))
        attn = merge_heads(attn_h)
        outputs.append(jnp.dot(attn, out_weight, preferred_element_type=jnp.float32).astype(jnp.bfloat16))
        weight_grad = weight_grad + jnp.dot(attn.T, cotangent[doc_index], preferred_element_type=jnp.float32)
        grads_q.append(merge_heads(gq_h))
        grads_k.append(merge_heads(gk_h))
        grads_v.append(merge_heads(gv_h))
    weight_grad = weight_grad * (1.0 / math.sqrt(DOCS * SEQLEN))
    return (jnp.stack(outputs), jnp.stack(grads_q), jnp.stack(grads_k), jnp.stack(grads_v), weight_grad)
```

```python
import functools
import math

import jax
import jax.numpy as jnp
from jax import lax
from jax.experimental import pallas as pl
from jax.experimental.pallas import tpu as pltpu
from jax.sharding import Mesh
from jax.sharding import PartitionSpec as P

HEAD_SIZE = 128
BLOCK_TOKENS = 64
SCALE = 1.0 / math.sqrt(HEAD_SIZE)
VMEM_LIMIT = 50 * 1024 * 1024
NEGATIVE = -1e30


def dot_nt(a, b):
    return lax.dot_general(a, b, (((1,), (1,)), ((), ())), preferred_element_type=jnp.float32)


def dot_nn(a, b):
    return lax.dot_general(a, b, (((1,), (0,)), ((), ())), preferred_element_type=jnp.float32)


def dot_tn(a, b):
    return lax.dot_general(a, b, (((0,), (0,)), ((), ())), preferred_element_type=jnp.float32)


def vmem():
    return pl.BlockSpec(memory_space=pltpu.VMEM)


def smem():
    return pl.BlockSpec(memory_space=pltpu.SMEM)


def column_of(chunk, lo_count, head_count):
    lo, h = chunk // head_count, chunk % head_count
    return (h * lo_count + lo) * HEAD_SIZE


def pack_kernel(lo_count, head_count, a_ref, b_ref, c_ref, out_ref):
    rows = a_ref.shape[0]
    for chunk in range(lo_count * head_count):
        col = column_of(chunk, lo_count, head_count)
        for j, ref in enumerate((a_ref, b_ref, c_ref)):
            out_ref[chunk, j * rows : (j + 1) * rows, :] = ref[:, col : col + HEAD_SIZE]


def unpack_kernel(lo_count, head_count, in_ref, a_ref, b_ref, c_ref):
    rows = a_ref.shape[0]
    for chunk in range(lo_count * head_count):
        col = column_of(chunk, lo_count, head_count)
        for j, ref in enumerate((a_ref, b_ref, c_ref)):
            ref[:, col : col + HEAD_SIZE] = in_ref[chunk, j * rows : (j + 1) * rows, :]


def load_chunks(packed_ref, dests):
    rows = packed_ref.shape[1] // 3

    def body(c, carry):
        at = pl.ds(pl.multiple_of(c * rows, rows), rows)
        for j, dest in enumerate(dests):
            if dest is not None:
                dest[at, :] = packed_ref[c, j * rows : (j + 1) * rows, :]
        return carry

    lax.fori_loop(0, packed_ref.shape[0], body, 0)


def block_at(ref, b):
    return ref[pl.ds(pl.multiple_of(b * BLOCK_TOKENS, BLOCK_TOKENS), BLOCK_TOKENS), :]


def slots_of(i, off_ref, idx_ref, rand_count, total):
    g = off_ref[0] + i
    ids = [jnp.maximum(g - 1, 0), g, jnp.minimum(g + 1, total - 1), jnp.int32(0)]
    ids += [idx_ref[i * rand_count + r] for r in range(rand_count)]
    return g, ids


def masked_scores(q, keys, g, total):
    s = dot_nt(q, keys) * SCALE
    col = lax.broadcasted_iota(jnp.int32, (1, keys.shape[0]), 1) // BLOCK_TOKENS
    dead = ((col == 0) & (g == 0)) | ((col == 2) & (g == total - 1))
    return jnp.where(dead, NEGATIVE, s)


def forward_kernel(
    rand_count, unroll, off_ref, idx_ref, packed_ref, attn_ref, q_s, k_s, v_s
):
    total = k_s.shape[0] // BLOCK_TOKENS
    load_chunks(packed_ref, (q_s, k_s, v_s))
    count = attn_ref.shape[0] // BLOCK_TOKENS

    def body(step, carry):
        results = []
        for u in range(unroll):
            i = step * unroll + u
            g, ids = slots_of(i, off_ref, idx_ref, rand_count, total)
            keys = jnp.concatenate([block_at(k_s, b) for b in ids], axis=0)
            vals = jnp.concatenate([block_at(v_s, b) for b in ids], axis=0)
            s = masked_scores(block_at(q_s, g), keys, g, total)
            e = jnp.exp(s - jnp.max(s, axis=-1, keepdims=True))
            l = jnp.sum(e, axis=-1, keepdims=True)
            results.append((i, (dot_nn(e.astype(jnp.bfloat16), vals) / l).astype(jnp.bfloat16)))
        for i, out in results:
            at = pl.ds(pl.multiple_of(i * BLOCK_TOKENS, BLOCK_TOKENS), BLOCK_TOKENS)
            attn_ref[at, :] = out
        return carry

    lax.fori_loop(0, count // unroll, body, 0)


def backward_kernel(
    rand_count, unroll, off_ref, idx_ref, packed_ref, attn_ref, grad_ref, out_ref,
    q_s, k_s, v_s, dq_s, dk_s, dv_s,
):
    total = k_s.shape[0] // BLOCK_TOKENS
    load_chunks(packed_ref, (q_s, k_s, v_s))
    dk_s[...] = jnp.zeros_like(dk_s)
    dv_s[...] = jnp.zeros_like(dv_s)
    count = attn_ref.shape[0] // BLOCK_TOKENS
    if count != total:
        dq_s[...] = jnp.zeros_like(dq_s)

    def body(step, carry):
        results = []
        for u in range(unroll):
            i = step * unroll + u
            g, ids = slots_of(i, off_ref, idx_ref, rand_count, total)
            keys = jnp.concatenate([block_at(k_s, b) for b in ids], axis=0)
            vals = jnp.concatenate([block_at(v_s, b) for b in ids], axis=0)
            q = block_at(q_s, g)
            do = block_at(grad_ref, i)
            attn = block_at(attn_ref, i)
            s = masked_scores(q, keys, g, total)
            e = jnp.exp(s - jnp.max(s, axis=-1, keepdims=True))
            p = e * (1.0 / jnp.sum(e, axis=-1, keepdims=True))
            dp = dot_nt(do, vals)
            delta = jnp.sum(
                do.astype(jnp.float32) * attn.astype(jnp.float32), axis=-1, keepdims=True
            )
            ds = (p * (dp - delta)).astype(jnp.bfloat16)
            dq = dot_nn(ds, keys) * SCALE
            dk = dot_tn(ds, q) * SCALE
            dv = dot_tn(p.astype(jnp.bfloat16), do)
            results.append((g, ids, dq, dk, dv))
        for g, ids, dq, dk, dv in results:
            at = pl.ds(pl.multiple_of(g * BLOCK_TOKENS, BLOCK_TOKENS), BLOCK_TOKENS)
            dq_s[at, :] = dq.astype(dq_s.dtype)
            for n, b in enumerate(ids):
                at = pl.ds(pl.multiple_of(b * BLOCK_TOKENS, BLOCK_TOKENS), BLOCK_TOKENS)
                part = slice(n * BLOCK_TOKENS, (n + 1) * BLOCK_TOKENS)
                dk_s[at, :] += dk[part]
                dv_s[at, :] += dv[part]
        return carry

    lax.fori_loop(0, count // unroll, body, 0)
    rows = out_ref.shape[1] // 3

    def store(c, carry):
        at = pl.ds(pl.multiple_of(c * rows, rows), rows)
        for j, ref in enumerate((dq_s, dk_s, dv_s)):
            out_ref[c, j * rows : (j + 1) * rows, :] = ref[at, :].astype(out_ref.dtype)
        return carry

    lax.fori_loop(0, out_ref.shape[0], store, 0)


def unroll_for(count, most):
    return max(u for u in range(1, most + 1) if count % u == 0)


def params():
    return pltpu.CompilerParams(vmem_limit_bytes=VMEM_LIMIT)


def per_device(queries, key_rows, values, rand_blocks, out_weight, cotangent):
    bf16, f32 = jnp.bfloat16, jnp.float32
    dp_count = lax.axis_size("dp")
    hi_count = lax.axis_size("hi")
    lo_count = lax.axis_size("lo")
    head_count = lax.axis_size("head")
    seq_count = hi_count * lo_count
    group = lo_count * head_count
    rows, width = queries.shape[1], queries.shape[2]
    range_rows = rows * head_count
    own_rows = rows * group
    rand_count = rand_blocks.shape[2]
    head_dim = HEAD_SIZE

    packed = pl.pallas_call(
        functools.partial(pack_kernel, lo_count, head_count),
        out_shape=jax.ShapeDtypeStruct((group, 3 * rows, head_dim), bf16),
        in_specs=[vmem()] * 3,
        out_specs=vmem(),
        compiler_params=params(),
        name="pack_heads",
    )(queries[0], key_rows[0], values[0])
    packed = lax.all_to_all(packed, ("lo", "head"), split_axis=0, concat_axis=0, tiled=True)
    if hi_count > 1:
        packed = lax.all_gather(packed, "hi", axis=0, tiled=True)
    ids = lax.all_to_all(
        jnp.transpose(rand_blocks, (1, 0, 2)), "lo", split_axis=0, concat_axis=0, tiled=True
    ).reshape(-1)
    block_count = own_rows // BLOCK_TOKENS
    offset = (lax.axis_index("hi") * block_count).astype(jnp.int32).reshape(1)
    all_rows = own_rows * hi_count
    held = pltpu.VMEM((all_rows, head_dim), bf16)
    summed = pltpu.VMEM((all_rows, head_dim), f32)
    pair = 2 * own_rows * 8 * BLOCK_TOKENS * head_dim

    cot_rows = lax.all_gather(cotangent[0], "head", axis=0, tiled=True)
    weight_heads = out_weight.reshape(lo_count, head_dim, width)
    grad_piece = jnp.einsum(
        "te,hde->htd", cot_rows, weight_heads, preferred_element_type=f32
    ).astype(bf16)
    grad_rows = lax.all_to_all(
        grad_piece, "lo", split_axis=0, concat_axis=0, tiled=True
    ).reshape(own_rows, head_dim)

    attn = pl.pallas_call(
        functools.partial(forward_kernel, rand_count, unroll_for(block_count, 4)),
        out_shape=jax.ShapeDtypeStruct((own_rows, head_dim), bf16),
        in_specs=[smem(), smem(), vmem()],
        out_specs=vmem(),
        scratch_shapes=[held] * 3,
        compiler_params=params(),
        cost_estimate=pl.CostEstimate(
            flops=8 * pair, bytes_accessed=4 * own_rows * head_dim * 2,
            transcendentals=own_rows * 8 * BLOCK_TOKENS,
        ),
        name="attention_forward",
    )(offset, ids, packed)

    attn_heads = lax.all_to_all(
        attn.reshape(lo_count, range_rows, head_dim), "lo", split_axis=0, concat_axis=0, tiled=True
    )
    weight_acc = jnp.einsum(
        "htd,te->hde", attn_heads, cot_rows, preferred_element_type=f32
    ).reshape(lo_count * head_dim, width)

    grads = pl.pallas_call(
        functools.partial(backward_kernel, rand_count, unroll_for(block_count, 2)),
        out_shape=jax.ShapeDtypeStruct(
            (group * hi_count, 3 * rows, head_dim), bf16 if hi_count == 1 else f32
        ),
        in_specs=[smem(), smem(), vmem(), vmem(), vmem()],
        out_specs=vmem(),
        scratch_shapes=[held] * 3 + [pltpu.VMEM((all_rows, head_dim), f32), summed, summed],
        compiler_params=params(),
        cost_estimate=pl.CostEstimate(
            flops=20 * pair, bytes_accessed=8 * own_rows * head_dim * 2,
            transcendentals=own_rows * 8 * BLOCK_TOKENS,
        ),
        name="attention_backward",
    )(offset, ids, packed, attn, grad_rows)

    half = weight_acc.shape[0] // dp_count
    dp_index = lax.axis_index("dp")
    own_half = lax.dynamic_slice_in_dim(weight_acc, dp_index * half, half, axis=0)
    other_half = lax.dynamic_slice_in_dim(weight_acc, (1 - dp_index) * half, half, axis=0)
    swapped = lax.ppermute(other_half.astype(bf16), "dp", [(0, 1), (1, 0)])
    half_sum = own_half + swapped.astype(f32)
    pieces = lax.all_to_all(
        half_sum.astype(bf16), ("hi", "lo"), split_axis=0, concat_axis=0, tiled=True
    ).reshape(seq_count, half // seq_count, width)
    token_total = dp_count * seq_count * range_rows
    piece = jnp.sum(pieces.astype(f32), axis=0) * (1.0 / math.sqrt(token_total))
    weight_grad = lax.all_gather(
        piece.astype(bf16), ("dp", "hi", "lo"), axis=0, tiled=True
    ).astype(f32)

    partial = jnp.einsum(
        "htd,hde->te", attn_heads, weight_heads, preferred_element_type=f32
    ).astype(bf16)
    parts = lax.all_to_all(partial, "head", split_axis=0, concat_axis=0, tiled=True)
    layer_out = jnp.sum(
        parts.reshape(head_count, rows, width).astype(f32), axis=0
    ).astype(bf16)

    if hi_count > 1:
        grads = lax.psum_scatter(grads, "hi", scatter_dimension=0, tiled=True).astype(bf16)
    returned = lax.all_to_all(grads, ("lo", "head"), split_axis=0, concat_axis=0, tiled=True)
    grad_q, grad_k, grad_v = pl.pallas_call(
        functools.partial(unpack_kernel, lo_count, head_count),
        out_shape=[jax.ShapeDtypeStruct((rows, width), bf16)] * 3,
        in_specs=[vmem()],
        out_specs=[vmem()] * 3,
        compiler_params=params(),
        name="unpack_heads",
    )(returned)
    return (layer_out[None], grad_q[None], grad_k[None], grad_v[None], weight_grad)


def solution(mesh):
    dp, seq, head = (mesh.shape[name] for name in ("dp", "seq", "head"))
    heads = 16
    lo = heads // head
    cut = Mesh(mesh.devices.reshape(dp, seq // lo, lo, head), ("dp", "hi", "lo", "head"))
    tokens = P("dp", ("hi", "lo", "head"), None)
    return jax.shard_map(
        per_device,
        mesh=cut,
        in_specs=(tokens, tokens, tokens, P(("hi", "lo"), "head", None), P("head", None), tokens),
        out_specs=(tokens, tokens, tokens, tokens, P("head", None)),
        check_vma=False,
    )
```

```python
import functools
import math

import jax
import jax.numpy as jnp
from jax import lax
from jax.experimental import pallas as pl
from jax.experimental.pallas import tpu as pltpu
from jax.sharding import Mesh
from jax.sharding import PartitionSpec as P

HEAD_SIZE = 128
BLOCK_TOKENS = 64
SCALE = 1.0 / math.sqrt(HEAD_SIZE)
VMEM_LIMIT = 50 * 1024 * 1024
NEGATIVE = -1e30


def dot_nt(a, b):
    return lax.dot_general(a, b, (((1,), (1,)), ((), ())), preferred_element_type=jnp.float32)


def dot_nn(a, b):
    return lax.dot_general(a, b, (((1,), (0,)), ((), ())), preferred_element_type=jnp.float32)


def dot_tn(a, b):
    return lax.dot_general(a, b, (((0,), (0,)), ((), ())), preferred_element_type=jnp.float32)


def vmem():
    return pl.BlockSpec(memory_space=pltpu.VMEM)


def smem():
    return pl.BlockSpec(memory_space=pltpu.SMEM)


def column_of(chunk, lo_count, head_count):
    lo, h = chunk // head_count, chunk % head_count
    return (h * lo_count + lo) * HEAD_SIZE


def pack_kernel(lo_count, head_count, a_ref, b_ref, c_ref, out_ref):
    rows = a_ref.shape[0]
    for chunk in range(lo_count * head_count):
        col = column_of(chunk, lo_count, head_count)
        for j, ref in enumerate((a_ref, b_ref, c_ref)):
            out_ref[chunk, j * rows : (j + 1) * rows, :] = ref[:, col : col + HEAD_SIZE]


def unpack_kernel(lo_count, head_count, in_ref, a_ref, b_ref, c_ref):
    rows = a_ref.shape[0]
    for chunk in range(lo_count * head_count):
        col = column_of(chunk, lo_count, head_count)
        for j, ref in enumerate((a_ref, b_ref, c_ref)):
            ref[:, col : col + HEAD_SIZE] = in_ref[chunk, j * rows : (j + 1) * rows, :]


def load_chunks(packed_ref, dests):
    rows = packed_ref.shape[1] // 3

    def body(c, carry):
        at = pl.ds(pl.multiple_of(c * rows, rows), rows)
        for j, dest in enumerate(dests):
            if dest is not None:
                dest[at, :] = packed_ref[c, j * rows : (j + 1) * rows, :]
        return carry

    lax.fori_loop(0, packed_ref.shape[0], body, 0)


def block_at(ref, b):
    return ref[pl.ds(pl.multiple_of(b * BLOCK_TOKENS, BLOCK_TOKENS), BLOCK_TOKENS), :]


def slots_of(i, off_ref, idx_ref, dims, total):
    lo_count, blocks, rand_count = dims
    g = off_ref[0] + i
    me = off_ref[1]
    piece = (i // blocks) ^ me
    base = ((piece * blocks + i % blocks) * lo_count + me) * rand_count
    ids = [jnp.maximum(g - 1, 0), g, jnp.minimum(g + 1, total - 1), jnp.int32(0)]
    ids += [idx_ref[base + r] for r in range(rand_count)]
    return g, ids


def masked_scores(q, keys, g, total):
    s = dot_nt(q, keys) * SCALE
    col = lax.broadcasted_iota(jnp.int32, (1, keys.shape[0]), 1) // BLOCK_TOKENS
    dead = ((col == 0) & (g == 0)) | ((col == 2) & (g == total - 1))
    return jnp.where(dead, NEGATIVE, s)


def forward_kernel(
    dims, unroll, off_ref, idx_ref, packed_ref, attn_ref, q_s, k_s, v_s
):
    total = k_s.shape[0] // BLOCK_TOKENS
    load_chunks(packed_ref, (q_s, k_s, v_s))
    count = attn_ref.shape[0] // BLOCK_TOKENS

    def body(step, carry):
        results = []
        for u in range(unroll):
            i = step * unroll + u
            g, ids = slots_of(i, off_ref, idx_ref, dims, total)
            keys = jnp.concatenate([block_at(k_s, b) for b in ids], axis=0)
            vals = jnp.concatenate([block_at(v_s, b) for b in ids], axis=0)
            s = masked_scores(block_at(q_s, g), keys, g, total)
            e = jnp.exp(s - jnp.max(s, axis=-1, keepdims=True))
            l = jnp.sum(e, axis=-1, keepdims=True)
            results.append((i, (dot_nn(e.astype(jnp.bfloat16), vals) / l).astype(jnp.bfloat16)))
        for i, out in results:
            at = pl.ds(pl.multiple_of(i * BLOCK_TOKENS, BLOCK_TOKENS), BLOCK_TOKENS)
            attn_ref[at, :] = out
        return carry

    lax.fori_loop(0, count // unroll, body, 0)


def backward_kernel(
    dims, unroll, off_ref, idx_ref, packed_ref, attn_ref, grad_ref, out_ref,
    q_s, k_s, v_s, dq_s, dk_s, dv_s,
):
    total = k_s.shape[0] // BLOCK_TOKENS
    load_chunks(packed_ref, (q_s, k_s, v_s))
    dk_s[...] = jnp.zeros_like(dk_s)
    dv_s[...] = jnp.zeros_like(dv_s)
    count = attn_ref.shape[0] // BLOCK_TOKENS
    if count != total:
        dq_s[...] = jnp.zeros_like(dq_s)

    def body(step, carry):
        results = []
        for u in range(unroll):
            i = step * unroll + u
            g, ids = slots_of(i, off_ref, idx_ref, dims, total)
            keys = jnp.concatenate([block_at(k_s, b) for b in ids], axis=0)
            vals = jnp.concatenate([block_at(v_s, b) for b in ids], axis=0)
            q = block_at(q_s, g)
            do = block_at(grad_ref, i)
            attn = block_at(attn_ref, i)
            s = masked_scores(q, keys, g, total)
            e = jnp.exp(s - jnp.max(s, axis=-1, keepdims=True))
            p = e * (1.0 / jnp.sum(e, axis=-1, keepdims=True))
            dp = dot_nt(do, vals)
            delta = jnp.sum(
                do.astype(jnp.float32) * attn.astype(jnp.float32), axis=-1, keepdims=True
            )
            ds = (p * (dp - delta)).astype(jnp.bfloat16)
            dq = dot_nn(ds, keys) * SCALE
            dk = dot_tn(ds, q) * SCALE
            dv = dot_tn(p.astype(jnp.bfloat16), do)
            results.append((g, ids, dq, dk, dv))
        for g, ids, dq, dk, dv in results:
            at = pl.ds(pl.multiple_of(g * BLOCK_TOKENS, BLOCK_TOKENS), BLOCK_TOKENS)
            dq_s[at, :] = dq.astype(dq_s.dtype)
            for n, b in enumerate(ids):
                at = pl.ds(pl.multiple_of(b * BLOCK_TOKENS, BLOCK_TOKENS), BLOCK_TOKENS)
                part = slice(n * BLOCK_TOKENS, (n + 1) * BLOCK_TOKENS)
                dk_s[at, :] += dk[part]
                dv_s[at, :] += dv[part]
        return carry

    lax.fori_loop(0, count // unroll, body, 0)
    rows = out_ref.shape[1] // 3

    def store(c, carry):
        at = pl.ds(pl.multiple_of(c * rows, rows), rows)
        for j, ref in enumerate((dq_s, dk_s, dv_s)):
            out_ref[c, j * rows : (j + 1) * rows, :] = ref[at, :].astype(out_ref.dtype)
        return carry

    lax.fori_loop(0, out_ref.shape[0], store, 0)


def unroll_for(count, most):
    return max(u for u in range(1, most + 1) if count % u == 0)


def swap_pieces(send, axis):
    count = lax.axis_size(axis)
    return [
        lax.ppermute(send(k), axis, [(i, i ^ k) for i in range(count)]) for k in range(1, count)
    ]


def chunk_for(x, index):
    return lax.dynamic_slice_in_dim(x, index, 1, axis=0)[0]


def scatter_sum(x, axis):
    count = lax.axis_size(axis)
    me = lax.axis_index(axis)
    x = x.reshape((count, x.shape[0] // count) + x.shape[1:])
    if count > 4:
        pieces = lax.all_to_all(
            x.astype(jnp.bfloat16), axis, split_axis=0, concat_axis=0, tiled=True
        )
        return jnp.sum(pieces.astype(jnp.float32), axis=0)
    total = chunk_for(x, me).astype(jnp.float32)
    for piece in swap_pieces(lambda k: chunk_for(x, me ^ k).astype(jnp.bfloat16), axis):
        total = total + piece.astype(jnp.float32)
    return total


def gather_rows(x, axis):
    rows = x.shape[0]
    me = lax.axis_index(axis)
    whole = jnp.zeros((rows * lax.axis_size(axis),) + x.shape[1:], x.dtype)
    for k, piece in enumerate([x] + swap_pieces(lambda k: x, axis)):
        whole = lax.dynamic_update_slice_in_dim(whole, piece, (me ^ k) * rows, axis=0)
    return whole


def params():
    return pltpu.CompilerParams(vmem_limit_bytes=VMEM_LIMIT)


def per_device(queries, key_rows, values, rand_blocks, out_weight, cotangent):
    bf16, f32 = jnp.bfloat16, jnp.float32
    dp_count = lax.axis_size("dp")
    hi_count = lax.axis_size("hi")
    lo_count = lax.axis_size("lo")
    head_count = lax.axis_size("head")
    seq_count = hi_count * lo_count
    group = lo_count * head_count
    rows, width = queries.shape[1], queries.shape[2]
    range_rows = rows * head_count
    own_rows = rows * group
    rand_count = rand_blocks.shape[2]
    head_dim = HEAD_SIZE

    packed = pl.pallas_call(
        functools.partial(pack_kernel, lo_count, head_count),
        out_shape=jax.ShapeDtypeStruct((group, 3 * rows, head_dim), bf16),
        in_specs=[vmem()] * 3,
        out_specs=vmem(),
        compiler_params=params(),
        name="pack_heads",
    )(queries[0], key_rows[0], values[0])
    packed = lax.all_to_all(packed, ("lo", "head"), split_axis=0, concat_axis=0, tiled=True)
    if hi_count > 1:
        packed = lax.all_gather(packed, "hi", axis=0, tiled=True)
    id_pieces = [rand_blocks] + swap_pieces(lambda k: rand_blocks, "lo")
    ids = jnp.stack(id_pieces).reshape(-1)
    dims = (lo_count, rand_blocks.shape[0], rand_count)
    block_count = own_rows // BLOCK_TOKENS
    offset = jnp.stack([lax.axis_index("hi") * block_count, lax.axis_index("lo")]).astype(jnp.int32)
    all_rows = own_rows * hi_count
    held = pltpu.VMEM((all_rows, head_dim), bf16)
    summed = pltpu.VMEM((all_rows, head_dim), f32)
    pair = 2 * own_rows * 8 * BLOCK_TOKENS * head_dim

    cot_rows = gather_rows(cotangent[0], "head")
    weight_heads = out_weight.reshape(lo_count, head_dim, width)
    grad_piece = jnp.einsum(
        "te,hde->htd", cot_rows, weight_heads, preferred_element_type=f32
    ).astype(bf16)
    packed, grad_piece = lax.optimization_barrier((packed, grad_piece))
    grad_rows = lax.all_to_all(
        grad_piece, "lo", split_axis=0, concat_axis=0, tiled=True
    ).reshape(own_rows, head_dim)

    attn = pl.pallas_call(
        functools.partial(forward_kernel, dims, unroll_for(block_count, 4)),
        out_shape=jax.ShapeDtypeStruct((own_rows, head_dim), bf16),
        in_specs=[smem(), smem(), vmem()],
        out_specs=vmem(),
        scratch_shapes=[held] * 3,
        compiler_params=params(),
        cost_estimate=pl.CostEstimate(
            flops=8 * pair, bytes_accessed=4 * own_rows * head_dim * 2,
            transcendentals=own_rows * 8 * BLOCK_TOKENS,
        ),
        name="attention_forward",
    )(offset, ids, packed)

    attn_heads = lax.all_to_all(
        attn.reshape(lo_count, range_rows, head_dim), "lo", split_axis=0, concat_axis=0, tiled=True
    )
    grads = pl.pallas_call(
        functools.partial(backward_kernel, dims, unroll_for(block_count, 4)),
        out_shape=jax.ShapeDtypeStruct(
            (group * hi_count, 3 * rows, head_dim), bf16 if hi_count == 1 else f32
        ),
        in_specs=[smem(), smem(), vmem(), vmem(), vmem()],
        out_specs=vmem(),
        scratch_shapes=[held] * 3 + [pltpu.VMEM((all_rows, head_dim), f32), summed, summed],
        compiler_params=params(),
        cost_estimate=pl.CostEstimate(
            flops=20 * pair, bytes_accessed=8 * own_rows * head_dim * 2,
            transcendentals=own_rows * 8 * BLOCK_TOKENS,
        ),
        name="attention_backward",
    )(offset, ids, packed, attn, grad_rows)

    attn_heads, grads = lax.optimization_barrier((attn_heads, grads))
    weight_acc = jnp.einsum(
        "htd,te->hde", attn_heads, cot_rows, preferred_element_type=f32
    ).reshape(lo_count * head_dim, width)

    half = weight_acc.shape[0] // dp_count
    dp_index = lax.axis_index("dp")
    own_half = lax.dynamic_slice_in_dim(weight_acc, dp_index * half, half, axis=0)
    other_half = lax.dynamic_slice_in_dim(weight_acc, (1 - dp_index) * half, half, axis=0)
    swapped = lax.ppermute(other_half.astype(bf16), "dp", [(0, 1), (1, 0)])
    half_sum = own_half + swapped.astype(f32)
    token_total = dp_count * seq_count * range_rows
    ranges = "lo" if hi_count == 1 else ("hi", "lo")
    piece = scatter_sum(half_sum, ranges) * (1.0 / math.sqrt(token_total))
    weight_grad = lax.all_gather(
        piece.astype(bf16), ("dp", "hi", "lo"), axis=0, tiled=True
    ).astype(f32)

    partial = jnp.einsum("htd,hde->te", attn_heads, weight_heads, preferred_element_type=f32)
    layer_out = scatter_sum(partial, "head").astype(bf16)

    if hi_count > 1:
        grads = lax.psum_scatter(grads, "hi", scatter_dimension=0, tiled=True).astype(bf16)
    returned = lax.all_to_all(grads, ("lo", "head"), split_axis=0, concat_axis=0, tiled=True)
    grad_q, grad_k, grad_v = pl.pallas_call(
        functools.partial(unpack_kernel, lo_count, head_count),
        out_shape=[jax.ShapeDtypeStruct((rows, width), bf16)] * 3,
        in_specs=[vmem()],
        out_specs=[vmem()] * 3,
        compiler_params=params(),
        name="unpack_heads",
    )(returned)
    return (layer_out[None], grad_q[None], grad_k[None], grad_v[None], weight_grad)


def solution(mesh):
    dp, seq, head = (mesh.shape[name] for name in ("dp", "seq", "head"))
    heads = 16
    lo = heads // head
    cut = Mesh(mesh.devices.reshape(dp, seq // lo, lo, head), ("dp", "hi", "lo", "head"))
    tokens = P("dp", ("hi", "lo", "head"), None)
    return jax.shard_map(
        per_device,
        mesh=cut,
        in_specs=(tokens, tokens, tokens, P(("hi", "lo"), "head", None), P("head", None), tokens),
        out_specs=(tokens, tokens, tokens, tokens, P("head", None)),
        check_vma=False,
    )
```

```python
import functools
import math

import jax
import jax.numpy as jnp
from jax import lax
from jax.experimental import pallas as pl
from jax.experimental.pallas import tpu as pltpu
from jax.sharding import Mesh
from jax.sharding import PartitionSpec as P

HEAD_SIZE = 128
BLOCK_TOKENS = 64
SCALE = 1.0 / math.sqrt(HEAD_SIZE)
VMEM_LIMIT = 50 * 1024 * 1024
NEGATIVE = -1e30


def dot_nt(a, b):
    return lax.dot_general(a, b, (((1,), (1,)), ((), ())), preferred_element_type=jnp.float32)


def dot_nn(a, b):
    return lax.dot_general(a, b, (((1,), (0,)), ((), ())), preferred_element_type=jnp.float32)


def dot_tn(a, b):
    return lax.dot_general(a, b, (((0,), (0,)), ((), ())), preferred_element_type=jnp.float32)


def vmem():
    return pl.BlockSpec(memory_space=pltpu.VMEM)


def smem():
    return pl.BlockSpec(memory_space=pltpu.SMEM)


def column_of(chunk, lo_count, head_count):
    lo, h = chunk // head_count, chunk % head_count
    return (h * lo_count + lo) * HEAD_SIZE


def pack_kernel(lo_count, head_count, a_ref, b_ref, c_ref, out_ref):
    rows = a_ref.shape[0]
    for chunk in range(lo_count * head_count):
        col = column_of(chunk, lo_count, head_count)
        for j, ref in enumerate((a_ref, b_ref, c_ref)):
            out_ref[chunk, j * rows : (j + 1) * rows, :] = ref[:, col : col + HEAD_SIZE]


def unpack_kernel(lo_count, head_count, in_ref, a_ref, b_ref, c_ref):
    rows = a_ref.shape[0]
    for chunk in range(lo_count * head_count):
        col = column_of(chunk, lo_count, head_count)
        for j, ref in enumerate((a_ref, b_ref, c_ref)):
            ref[:, col : col + HEAD_SIZE] = in_ref[chunk, j * rows : (j + 1) * rows, :]


def load_chunks(packed_ref, dests):
    rows = packed_ref.shape[1] // 3

    def body(c, carry):
        at = pl.ds(pl.multiple_of(c * rows, rows), rows)
        for j, dest in enumerate(dests):
            if dest is not None:
                dest[at, :] = packed_ref[c, j * rows : (j + 1) * rows, :]
        return carry

    lax.fori_loop(0, packed_ref.shape[0], body, 0)


def block_at(ref, b):
    return ref[pl.ds(pl.multiple_of(b * BLOCK_TOKENS, BLOCK_TOKENS), BLOCK_TOKENS), :]


def slots_of(i, off_ref, idx_ref, dims, total):
    lo_count, rand_count = dims
    g = off_ref[0] + i
    me = off_ref[1]
    base = (i * lo_count + me) * rand_count
    ids = [jnp.maximum(g - 1, 0), g, jnp.minimum(g + 1, total - 1), jnp.int32(0)]
    ids += [idx_ref[base + r] for r in range(rand_count)]
    return g, ids


def masked_scores(q, keys, g, total):
    s = dot_nt(q, keys) * SCALE
    col = lax.broadcasted_iota(jnp.int32, (1, keys.shape[0]), 1) // BLOCK_TOKENS
    dead = ((col == 0) & (g == 0)) | ((col == 2) & (g == total - 1))
    return jnp.where(dead, NEGATIVE, s)


def forward_kernel(
    dims, unroll, off_ref, idx_ref, packed_ref, attn_ref, q_s, k_s, v_s
):
    total = k_s.shape[0] // BLOCK_TOKENS
    load_chunks(packed_ref, (q_s, k_s, v_s))
    count = attn_ref.shape[0] // BLOCK_TOKENS

    def body(step, carry):
        results = []
        for u in range(unroll):
            i = step * unroll + u
            g, ids = slots_of(i, off_ref, idx_ref, dims, total)
            keys = jnp.concatenate([block_at(k_s, b) for b in ids], axis=0)
            vals = jnp.concatenate([block_at(v_s, b) for b in ids], axis=0)
            s = masked_scores(block_at(q_s, g), keys, g, total)
            e = jnp.exp(s - jnp.max(s, axis=-1, keepdims=True))
            l = jnp.sum(e, axis=-1, keepdims=True)
            results.append((i, (dot_nn(e.astype(jnp.bfloat16), vals) / l).astype(jnp.bfloat16)))
        for i, out in results:
            at = pl.ds(pl.multiple_of(i * BLOCK_TOKENS, BLOCK_TOKENS), BLOCK_TOKENS)
            attn_ref[at, :] = out
        return carry

    lax.fori_loop(0, count // unroll, body, 0)


def backward_kernel(
    dims, unroll, off_ref, idx_ref, packed_ref, attn_ref, grad_ref, out_ref,
    q_s, k_s, v_s, dq_s, dk_s, dv_s,
):
    total = k_s.shape[0] // BLOCK_TOKENS
    load_chunks(packed_ref, (q_s, k_s, v_s))
    dk_s[...] = jnp.zeros_like(dk_s)
    dv_s[...] = jnp.zeros_like(dv_s)
    count = attn_ref.shape[0] // BLOCK_TOKENS
    if count != total:
        dq_s[...] = jnp.zeros_like(dq_s)

    def body(step, carry):
        results = []
        for u in range(unroll):
            i = step * unroll + u
            g, ids = slots_of(i, off_ref, idx_ref, dims, total)
            keys = jnp.concatenate([block_at(k_s, b) for b in ids], axis=0)
            vals = jnp.concatenate([block_at(v_s, b) for b in ids], axis=0)
            q = block_at(q_s, g)
            do = block_at(grad_ref, i)
            attn = block_at(attn_ref, i)
            s = masked_scores(q, keys, g, total)
            e = jnp.exp(s - jnp.max(s, axis=-1, keepdims=True))
            p = e * (1.0 / jnp.sum(e, axis=-1, keepdims=True))
            dp = dot_nt(do, vals)
            delta = jnp.sum(
                do.astype(jnp.float32) * attn.astype(jnp.float32), axis=-1, keepdims=True
            )
            ds = (p * (dp - delta)).astype(jnp.bfloat16)
            dq = dot_nn(ds, keys) * SCALE
            dk = dot_tn(ds, q) * SCALE
            dv = dot_tn(p.astype(jnp.bfloat16), do)
            results.append((g, ids, dq, dk, dv))
        for g, ids, dq, dk, dv in results:
            at = pl.ds(pl.multiple_of(g * BLOCK_TOKENS, BLOCK_TOKENS), BLOCK_TOKENS)
            dq_s[at, :] = dq.astype(dq_s.dtype)
            for n, b in enumerate(ids):
                at = pl.ds(pl.multiple_of(b * BLOCK_TOKENS, BLOCK_TOKENS), BLOCK_TOKENS)
                part = slice(n * BLOCK_TOKENS, (n + 1) * BLOCK_TOKENS)
                dk_s[at, :] += dk[part]
                dv_s[at, :] += dv[part]
        return carry

    lax.fori_loop(0, count // unroll, body, 0)
    rows = out_ref.shape[1] // 3

    def store(c, carry):
        at = pl.ds(pl.multiple_of(c * rows, rows), rows)
        for j, ref in enumerate((dq_s, dk_s, dv_s)):
            out_ref[c, j * rows : (j + 1) * rows, :] = ref[at, :].astype(out_ref.dtype)
        return carry

    lax.fori_loop(0, out_ref.shape[0], store, 0)


def unroll_for(count, most):
    return max(u for u in range(1, most + 1) if count % u == 0)


def swap_pieces(send, axis):
    count = lax.axis_size(axis)
    return [
        lax.ppermute(send(k), axis, [(i, i ^ k) for i in range(count)]) for k in range(1, count)
    ]


def chunk_for(x, index):
    return lax.dynamic_slice_in_dim(x, index, 1, axis=0)[0]


def scatter_sum(x, axis):
    count = lax.axis_size(axis)
    me = lax.axis_index(axis)
    x = x.reshape((count, x.shape[0] // count) + x.shape[1:])
    if count > 4:
        pieces = lax.all_to_all(
            x.astype(jnp.bfloat16), axis, split_axis=0, concat_axis=0, tiled=True
        )
        return jnp.sum(pieces.astype(jnp.float32), axis=0)
    total = chunk_for(x, me).astype(jnp.float32)
    for piece in swap_pieces(lambda k: chunk_for(x, me ^ k).astype(jnp.bfloat16), axis):
        total = total + piece.astype(jnp.float32)
    return total


def gather_rows(x, axis):
    rows = x.shape[0]
    me = lax.axis_index(axis)
    whole = jnp.zeros((rows * lax.axis_size(axis),) + x.shape[1:], x.dtype)
    for k, piece in enumerate([x] + swap_pieces(lambda k: x, axis)):
        whole = lax.dynamic_update_slice_in_dim(whole, piece, (me ^ k) * rows, axis=0)
    return whole


def params():
    return pltpu.CompilerParams(vmem_limit_bytes=VMEM_LIMIT)


def per_device(queries, key_rows, values, rand_blocks, out_weight, cotangent):
    bf16, f32 = jnp.bfloat16, jnp.float32
    dp_count = lax.axis_size("dp")
    hi_count = lax.axis_size("hi")
    lo_count = lax.axis_size("lo")
    head_count = lax.axis_size("head")
    seq_count = hi_count * lo_count
    group = lo_count * head_count
    rows, width = queries.shape[1], queries.shape[2]
    range_rows = rows * head_count
    own_rows = rows * group
    rand_count = rand_blocks.shape[2]
    head_dim = HEAD_SIZE

    packed = pl.pallas_call(
        functools.partial(pack_kernel, lo_count, head_count),
        out_shape=jax.ShapeDtypeStruct((group, 3 * rows, head_dim), bf16),
        in_specs=[vmem()] * 3,
        out_specs=vmem(),
        compiler_params=params(),
        name="pack_heads",
    )(queries[0], key_rows[0], values[0])
    packed = lax.all_to_all(packed, ("lo", "head"), split_axis=0, concat_axis=0, tiled=True)
    if hi_count > 1:
        packed = lax.all_gather(packed, "hi", axis=0, tiled=True)
    ids = lax.all_gather(rand_blocks, "lo", axis=0, tiled=True).reshape(-1)
    dims = (lo_count, rand_count)
    block_count = own_rows // BLOCK_TOKENS
    offset = jnp.stack([lax.axis_index("hi") * block_count, lax.axis_index("lo")]).astype(jnp.int32)
    all_rows = own_rows * hi_count
    held = pltpu.VMEM((all_rows, head_dim), bf16)
    summed = pltpu.VMEM((all_rows, head_dim), f32)
    pair = 2 * own_rows * 8 * BLOCK_TOKENS * head_dim

    cot_rows = gather_rows(cotangent[0], "head")
    weight_heads = out_weight.reshape(lo_count, head_dim, width)
    grad_piece = jnp.einsum(
        "te,hde->htd", cot_rows, weight_heads, preferred_element_type=f32
    ).astype(bf16)
    attn = pl.pallas_call(
        functools.partial(forward_kernel, dims, unroll_for(block_count, 4)),
        out_shape=jax.ShapeDtypeStruct((own_rows, head_dim), bf16),
        in_specs=[smem(), smem(), vmem()],
        out_specs=vmem(),
        scratch_shapes=[held] * 3,
        compiler_params=params(),
        cost_estimate=pl.CostEstimate(
            flops=8 * pair, bytes_accessed=4 * own_rows * head_dim * 2,
            transcendentals=own_rows * 8 * BLOCK_TOKENS,
        ),
        name="attention_forward",
    )(offset, ids, packed)

    attn_heads = lax.all_to_all(
        attn.reshape(lo_count, range_rows, head_dim), "lo", split_axis=0, concat_axis=0, tiled=True
    )
    attn_heads, grad_piece = lax.optimization_barrier((attn_heads, grad_piece))
    grad_rows = lax.all_to_all(
        grad_piece, "lo", split_axis=0, concat_axis=0, tiled=True
    ).reshape(own_rows, head_dim)
    weight_acc = jnp.einsum(
        "htd,te->hde", attn_heads, cot_rows, preferred_element_type=f32
    ).reshape(lo_count * head_dim, width)

    half = weight_acc.shape[0] // dp_count
    dp_index = lax.axis_index("dp")
    own_half = lax.dynamic_slice_in_dim(weight_acc, dp_index * half, half, axis=0)
    other_half = lax.dynamic_slice_in_dim(weight_acc, (1 - dp_index) * half, half, axis=0)
    swapped = lax.ppermute(other_half.astype(bf16), "dp", [(0, 1), (1, 0)])
    half_sum = own_half + swapped.astype(f32)
    partial = jnp.einsum("htd,hde->te", attn_heads, weight_heads, preferred_element_type=f32)
    grad_rows, half_sum, partial = lax.optimization_barrier((grad_rows, half_sum, partial))
    grads = pl.pallas_call(
        functools.partial(backward_kernel, dims, unroll_for(block_count, 4)),
        out_shape=jax.ShapeDtypeStruct(
            (group * hi_count, 3 * rows, head_dim), bf16 if hi_count == 1 else f32
        ),
        in_specs=[smem(), smem(), vmem(), vmem(), vmem()],
        out_specs=vmem(),
        scratch_shapes=[held] * 3 + [pltpu.VMEM((all_rows, head_dim), f32), summed, summed],
        compiler_params=params(),
        cost_estimate=pl.CostEstimate(
            flops=20 * pair, bytes_accessed=8 * own_rows * head_dim * 2,
            transcendentals=own_rows * 8 * BLOCK_TOKENS,
        ),
        name="attention_backward",
    )(offset, ids, packed, attn, grad_rows)

    token_total = dp_count * seq_count * range_rows
    ranges = "lo" if hi_count == 1 else ("hi", "lo")
    piece = scatter_sum(half_sum, ranges) * (1.0 / math.sqrt(token_total))
    mine = lax.all_gather(piece.astype(bf16), ranges, axis=0, tiled=True)
    other = lax.ppermute(mine, "dp", [(0, 1), (1, 0)])
    weight_grad = jnp.where(
        dp_index == 0, jnp.concatenate([mine, other]), jnp.concatenate([other, mine])
    ).astype(f32)
    layer_out = scatter_sum(partial, "head").astype(bf16)

    if hi_count > 1:
        grads = lax.psum_scatter(grads, "hi", scatter_dimension=0, tiled=True).astype(bf16)
    returned = lax.all_to_all(grads, ("lo", "head"), split_axis=0, concat_axis=0, tiled=True)
    grad_q, grad_k, grad_v = pl.pallas_call(
        functools.partial(unpack_kernel, lo_count, head_count),
        out_shape=[jax.ShapeDtypeStruct((rows, width), bf16)] * 3,
        in_specs=[vmem()],
        out_specs=[vmem()] * 3,
        compiler_params=params(),
        name="unpack_heads",
    )(returned)
    return (layer_out[None], grad_q[None], grad_k[None], grad_v[None], weight_grad)


def solution(mesh):
    dp, seq, head = (mesh.shape[name] for name in ("dp", "seq", "head"))
    heads = 16
    lo = heads // head
    cut = Mesh(mesh.devices.reshape(dp, seq // lo, lo, head), ("dp", "hi", "lo", "head"))
    tokens = P("dp", ("hi", "lo", "head"), None)
    return jax.shard_map(
        per_device,
        mesh=cut,
        in_specs=(tokens, tokens, tokens, P(("hi", "lo"), "head", None), P("head", None), tokens),
        out_specs=(tokens, tokens, tokens, tokens, P("head", None)),
        check_vma=False,
    )
```

```python
import functools
import math

import jax
import jax.numpy as jnp
from jax import lax
from jax.experimental import pallas as pl
from jax.experimental.pallas import tpu as pltpu
from jax.sharding import Mesh
from jax.sharding import PartitionSpec as P

HEAD_SIZE = 128
BLOCK_TOKENS = 64
SCALE = 1.0 / math.sqrt(HEAD_SIZE)
VMEM_LIMIT = 50 * 1024 * 1024
NEGATIVE = -1e30


def dot_nt(a, b):
    return lax.dot_general(a, b, (((1,), (1,)), ((), ())), preferred_element_type=jnp.float32)


def dot_nn(a, b):
    return lax.dot_general(a, b, (((1,), (0,)), ((), ())), preferred_element_type=jnp.float32)


def dot_tn(a, b):
    return lax.dot_general(a, b, (((0,), (0,)), ((), ())), preferred_element_type=jnp.float32)


def vmem():
    return pl.BlockSpec(memory_space=pltpu.VMEM)


def smem():
    return pl.BlockSpec(memory_space=pltpu.SMEM)


def column_of(chunk, lo_count, head_count):
    lo, h = chunk // head_count, chunk % head_count
    return (h * lo_count + lo) * HEAD_SIZE


def pack_kernel(lo_count, head_count, a_ref, b_ref, c_ref, out_ref):
    rows = a_ref.shape[0]
    for chunk in range(lo_count * head_count):
        col = column_of(chunk, lo_count, head_count)
        for j, ref in enumerate((a_ref, b_ref, c_ref)):
            out_ref[chunk, j * rows : (j + 1) * rows, :] = ref[:, col : col + HEAD_SIZE]


def unpack_kernel(lo_count, head_count, in_ref, a_ref, b_ref, c_ref):
    rows = a_ref.shape[0]
    for chunk in range(lo_count * head_count):
        col = column_of(chunk, lo_count, head_count)
        for j, ref in enumerate((a_ref, b_ref, c_ref)):
            ref[:, col : col + HEAD_SIZE] = in_ref[chunk, j * rows : (j + 1) * rows, :]


def load_chunks(packed_ref, dests):
    rows = packed_ref.shape[1] // 3

    def body(c, carry):
        at = pl.ds(pl.multiple_of(c * rows, rows), rows)
        for j, dest in enumerate(dests):
            if dest is not None:
                dest[at, :] = packed_ref[c, j * rows : (j + 1) * rows, :]
        return carry

    lax.fori_loop(0, packed_ref.shape[0], body, 0)


def block_at(ref, b):
    return ref[pl.ds(pl.multiple_of(b * BLOCK_TOKENS, BLOCK_TOKENS), BLOCK_TOKENS), :]


def slots_of(i, off_ref, idx_ref, dims, total):
    lo_count, blocks, rand_count = dims
    g = off_ref[0] + i
    me = off_ref[1]
    piece = (i // blocks) ^ me
    base = ((piece * blocks + i % blocks) * lo_count + me) * rand_count
    ids = [jnp.maximum(g - 1, 0), g, jnp.minimum(g + 1, total - 1), jnp.int32(0)]
    ids += [idx_ref[base + r] for r in range(rand_count)]
    return g, ids


def masked_scores(q, keys, g, total):
    s = dot_nt(q, keys) * SCALE
    col = lax.broadcasted_iota(jnp.int32, (1, keys.shape[0]), 1) // BLOCK_TOKENS
    dead = ((col == 0) & (g == 0)) | ((col == 2) & (g == total - 1))
    return jnp.where(dead, NEGATIVE, s)


def forward_kernel(
    dims, unroll, off_ref, idx_ref, packed_ref, attn_ref, q_s, k_s, v_s
):
    total = k_s.shape[0] // BLOCK_TOKENS
    load_chunks(packed_ref, (q_s, k_s, v_s))
    count = attn_ref.shape[0] // BLOCK_TOKENS

    def body(step, carry):
        results = []
        for u in range(unroll):
            i = step * unroll + u
            g, ids = slots_of(i, off_ref, idx_ref, dims, total)
            keys = jnp.concatenate([block_at(k_s, b) for b in ids], axis=0)
            vals = jnp.concatenate([block_at(v_s, b) for b in ids], axis=0)
            s = masked_scores(block_at(q_s, g), keys, g, total)
            e = jnp.exp(s - jnp.max(s, axis=-1, keepdims=True))
            l = jnp.sum(e, axis=-1, keepdims=True)
            results.append((i, (dot_nn(e.astype(jnp.bfloat16), vals) / l).astype(jnp.bfloat16)))
        for i, out in results:
            at = pl.ds(pl.multiple_of(i * BLOCK_TOKENS, BLOCK_TOKENS), BLOCK_TOKENS)
            attn_ref[at, :] = out
        return carry

    lax.fori_loop(0, count // unroll, body, 0)


def backward_kernel(
    dims, unroll, off_ref, idx_ref, packed_ref, attn_ref, grad_ref, out_ref,
    q_s, k_s, v_s, dq_s, dk_s, dv_s,
):
    total = k_s.shape[0] // BLOCK_TOKENS
    load_chunks(packed_ref, (q_s, k_s, v_s))
    dk_s[...] = jnp.zeros_like(dk_s)
    dv_s[...] = jnp.zeros_like(dv_s)
    count = attn_ref.shape[0] // BLOCK_TOKENS
    if count != total:
        dq_s[...] = jnp.zeros_like(dq_s)

    def body(step, carry):
        results = []
        for u in range(unroll):
            i = step * unroll + u
            g, ids = slots_of(i, off_ref, idx_ref, dims, total)
            keys = jnp.concatenate([block_at(k_s, b) for b in ids], axis=0)
            vals = jnp.concatenate([block_at(v_s, b) for b in ids], axis=0)
            q = block_at(q_s, g)
            do = block_at(grad_ref, i)
            attn = block_at(attn_ref, i)
            s = masked_scores(q, keys, g, total)
            e = jnp.exp(s - jnp.max(s, axis=-1, keepdims=True))
            p = e * (1.0 / jnp.sum(e, axis=-1, keepdims=True))
            dp = dot_nt(do, vals)
            delta = jnp.sum(
                do.astype(jnp.float32) * attn.astype(jnp.float32), axis=-1, keepdims=True
            )
            ds = (p * (dp - delta)).astype(jnp.bfloat16)
            dq = dot_nn(ds, keys) * SCALE
            dk = dot_tn(ds, q) * SCALE
            dv = dot_tn(p.astype(jnp.bfloat16), do)
            results.append((g, ids, dq, dk, dv))
        for g, ids, dq, dk, dv in results:
            at = pl.ds(pl.multiple_of(g * BLOCK_TOKENS, BLOCK_TOKENS), BLOCK_TOKENS)
            dq_s[at, :] = dq.astype(dq_s.dtype)
            for n, b in enumerate(ids):
                at = pl.ds(pl.multiple_of(b * BLOCK_TOKENS, BLOCK_TOKENS), BLOCK_TOKENS)
                part = slice(n * BLOCK_TOKENS, (n + 1) * BLOCK_TOKENS)
                dk_s[at, :] += dk[part]
                dv_s[at, :] += dv[part]
        return carry

    lax.fori_loop(0, count // unroll, body, 0)
    rows = out_ref.shape[1] // 3

    def store(c, carry):
        at = pl.ds(pl.multiple_of(c * rows, rows), rows)
        for j, ref in enumerate((dq_s, dk_s, dv_s)):
            out_ref[c, j * rows : (j + 1) * rows, :] = ref[at, :].astype(out_ref.dtype)
        return carry

    lax.fori_loop(0, out_ref.shape[0], store, 0)


def unroll_for(count, most):
    return max(u for u in range(1, most + 1) if count % u == 0)


def swap_pieces(pieces, axis):
    count = lax.axis_size(axis)
    return [
        lax.ppermute(piece, axis, [(i, i ^ k) for i in range(count)])
        for k, piece in enumerate(pieces, 1)
    ]


def chunk_for(x, index):
    return lax.dynamic_slice_in_dim(x, index, 1, axis=0)[0]


def cut_terms(x, axis):
    count = lax.axis_size(axis)
    me = lax.axis_index(axis)
    x = x.reshape((count, x.shape[0] // count) + x.shape[1:])
    if count > 4:
        return (x.astype(jnp.bfloat16),)
    return (chunk_for(x, me),) + tuple(
        chunk_for(x, me ^ k).astype(jnp.bfloat16) for k in range(1, count)
    )


def sum_terms(terms, axis):
    if len(terms) == 1:
        pieces = lax.all_to_all(terms[0], axis, split_axis=0, concat_axis=0, tiled=True)
        return jnp.sum(pieces.astype(jnp.float32), axis=0)
    total = terms[0].astype(jnp.float32)
    for piece in swap_pieces(terms[1:], axis):
        total = total + piece.astype(jnp.float32)
    return total


def params():
    return pltpu.CompilerParams(vmem_limit_bytes=VMEM_LIMIT)


def per_device(queries, key_rows, values, rand_blocks, out_weight, cotangent):
    bf16, f32 = jnp.bfloat16, jnp.float32
    dp_count = lax.axis_size("dp")
    hi_count = lax.axis_size("hi")
    lo_count = lax.axis_size("lo")
    head_count = lax.axis_size("head")
    seq_count = hi_count * lo_count
    group = lo_count * head_count
    rows, width = queries.shape[1], queries.shape[2]
    range_rows = rows * head_count
    own_rows = rows * group
    rand_count = rand_blocks.shape[2]
    head_dim = HEAD_SIZE

    packed = pl.pallas_call(
        functools.partial(pack_kernel, lo_count, head_count),
        out_shape=jax.ShapeDtypeStruct((group, 3 * rows, head_dim), bf16),
        in_specs=[vmem()] * 3,
        out_specs=vmem(),
        compiler_params=params(),
        name="pack_heads",
    )(queries[0], key_rows[0], values[0])
    packed = lax.all_to_all(packed, ("lo", "head"), split_axis=0, concat_axis=0, tiled=True)
    if hi_count > 1:
        packed = lax.all_gather(packed, "hi", axis=0, tiled=True)
    id_pieces = [rand_blocks] + swap_pieces([rand_blocks] * (lo_count - 1), "lo")
    ids = jnp.stack(id_pieces).reshape(-1)
    dims = (lo_count, rand_blocks.shape[0], rand_count)
    block_count = own_rows // BLOCK_TOKENS
    offset = jnp.stack([lax.axis_index("hi") * block_count, lax.axis_index("lo")]).astype(jnp.int32)
    all_rows = own_rows * hi_count
    held = pltpu.VMEM((all_rows, head_dim), bf16)
    summed = pltpu.VMEM((all_rows, head_dim), f32)
    pair = 2 * own_rows * 8 * BLOCK_TOKENS * head_dim

    cot_rows = lax.all_gather(cotangent[0], "head", axis=0, tiled=True)
    weight_heads = out_weight.reshape(lo_count, head_dim, width)
    grad_piece = jnp.einsum(
        "te,hde->htd", cot_rows, weight_heads, preferred_element_type=f32
    ).astype(bf16)
    attn = pl.pallas_call(
        functools.partial(forward_kernel, dims, unroll_for(block_count, 4)),
        out_shape=jax.ShapeDtypeStruct((own_rows, head_dim), bf16),
        in_specs=[smem(), smem(), vmem()],
        out_specs=vmem(),
        scratch_shapes=[held] * 3,
        compiler_params=params(),
        cost_estimate=pl.CostEstimate(
            flops=8 * pair, bytes_accessed=4 * own_rows * head_dim * 2,
            transcendentals=own_rows * 8 * BLOCK_TOKENS,
        ),
        name="attention_forward",
    )(offset, ids, packed)

    attn_heads = lax.all_to_all(
        attn.reshape(lo_count, range_rows, head_dim), "lo", split_axis=0, concat_axis=0, tiled=True
    )
    attn_heads, grad_piece = lax.optimization_barrier((attn_heads, grad_piece))
    grad_rows = lax.all_to_all(
        grad_piece, "lo", split_axis=0, concat_axis=0, tiled=True
    ).reshape(own_rows, head_dim)
    weight_acc = jnp.einsum(
        "htd,te->hde", attn_heads, cot_rows, preferred_element_type=f32
    ).reshape(lo_count * head_dim, width)

    half = weight_acc.shape[0] // dp_count
    dp_index = lax.axis_index("dp")
    own_half = lax.dynamic_slice_in_dim(weight_acc, dp_index * half, half, axis=0)
    other_half = lax.dynamic_slice_in_dim(weight_acc, (1 - dp_index) * half, half, axis=0)
    swapped = lax.ppermute(other_half.astype(bf16), "dp", [(0, 1), (1, 0)])
    half_sum = own_half + swapped.astype(f32)
    partial = jnp.einsum("htd,hde->te", attn_heads, weight_heads, preferred_element_type=f32)
    ranges = "lo" if hi_count == 1 else ("hi", "lo")
    weight_terms = cut_terms(half_sum, ranges)
    out_terms = cut_terms(partial, "head")
    grad_rows, weight_terms, out_terms = lax.optimization_barrier(
        (grad_rows, weight_terms, out_terms)
    )
    grads = pl.pallas_call(
        functools.partial(backward_kernel, dims, unroll_for(block_count, 4)),
        out_shape=jax.ShapeDtypeStruct(
            (group * hi_count, 3 * rows, head_dim), bf16 if hi_count == 1 else f32
        ),
        in_specs=[smem(), smem(), vmem(), vmem(), vmem()],
        out_specs=vmem(),
        scratch_shapes=[held] * 3 + [pltpu.VMEM((all_rows, head_dim), f32), summed, summed],
        compiler_params=params(),
        cost_estimate=pl.CostEstimate(
            flops=20 * pair, bytes_accessed=8 * own_rows * head_dim * 2,
            transcendentals=own_rows * 8 * BLOCK_TOKENS,
        ),
        name="attention_backward",
    )(offset, ids, packed, attn, grad_rows)

    token_total = dp_count * seq_count * range_rows
    piece = sum_terms(weight_terms, ranges) * (1.0 / math.sqrt(token_total))
    mine = lax.all_gather(piece.astype(bf16), ranges, axis=0, tiled=True)
    other = lax.ppermute(mine, "dp", [(0, 1), (1, 0)])
    weight_grad = jnp.where(
        dp_index == 0, jnp.concatenate([mine, other]), jnp.concatenate([other, mine])
    ).astype(f32)
    layer_out = sum_terms(out_terms, "head").astype(bf16)

    if hi_count > 1:
        grads = lax.psum_scatter(grads, "hi", scatter_dimension=0, tiled=True).astype(bf16)
    returned = lax.all_to_all(grads, ("lo", "head"), split_axis=0, concat_axis=0, tiled=True)
    grad_q, grad_k, grad_v = pl.pallas_call(
        functools.partial(unpack_kernel, lo_count, head_count),
        out_shape=[jax.ShapeDtypeStruct((rows, width), bf16)] * 3,
        in_specs=[vmem()],
        out_specs=[vmem()] * 3,
        compiler_params=params(),
        name="unpack_heads",
    )(returned)
    return (layer_out[None], grad_q[None], grad_k[None], grad_v[None], weight_grad)


def solution(mesh):
    dp, seq, head = (mesh.shape[name] for name in ("dp", "seq", "head"))
    heads = 16
    lo = heads // head
    cut = Mesh(mesh.devices.reshape(dp, seq // lo, lo, head), ("dp", "hi", "lo", "head"))
    tokens = P("dp", ("hi", "lo", "head"), None)
    return jax.shard_map(
        per_device,
        mesh=cut,
        in_specs=(tokens, tokens, tokens, P(("hi", "lo"), "head", None), P("head", None), tokens),
        out_specs=(tokens, tokens, tokens, tokens, P("head", None)),
        check_vma=False,
    )
```
